256 devices in a mesh: view: 8 (over y, x_hi), seq: 32 (over x_lo, z, core).
Axes of the slice: x: 4 (x_hi: 2, x_lo: 2; x = x_hi * 2 + x_lo), y: 4, z: 8, core: 2. Of those that a mesh axis runs over, the one named last changes fastest.
Arguments:
- queries: bfloat16 [8, 4096, 1536], P('view', 'seq'), may hold values from -10 to 10
- keys: bfloat16 [8, 4096, 1536], P('view', 'seq'), may hold values from -10 to 10
- values: bfloat16 [8, 4096, 1536], P('view', 'seq'), may hold values from -6 to 6
- hidden_in: bfloat16 [8, 4096, 1536], P('view', 'seq'), may hold values from -6 to 6
- gate: float32 [8, 1536], P('view'), may hold values from 0.5 to 1.5
- w_out: bfloat16 [1536, 1536], replicated, may hold values from -0.15625 to 0.15625
Outputs:
- block_out: bfloat16 [8, 4096, 1536], P('view', 'seq')
The draws below stay inside these ranges and needn't reach their ends.
All inputs are finite; a program needn't handle non-finite values.
Results may differ from the reference program's by a relative error of at most 0.0013.
The reference program's roundings to bfloat16 on the way count: a program that leaves them out, or rounds other values in their place, can miss the bound.
Values may be sent and summed in bfloat16 or wider, within the bound.
No kernel may reach another device: no remote copies, remote signals or barrier semaphores. Data moves between devices by JAX's collectives and lax.ppermute only.
A program may use at most 128 MiB of HBM per device.

```python
import jax
import jax.numpy as jnp
from jax import lax

HEADS = 24
HEAD_DIM = 64
D = 1536
VIEWS = 8
LEN = 4096


def draw_queries(key, part):
    key = jax.random.fold_in(key, 11)
    base = jnp.clip(1.4 * jax.random.normal(key, (VIEWS, LEN, D), jnp.float32), -8.0, 8.0)
    return base.astype(jnp.bfloat16)


def draw_keys(key, part):
    key = jax.random.fold_in(key, 23)
    base = jnp.clip(1.4 * jax.random.normal(key, (VIEWS, LEN, D), jnp.float32), -8.0, 8.0)
    return base.astype(jnp.bfloat16)


def shard_levels(stream_key, dims, cuts, least, high):
    factor_of = 1.0
    for axis_at, shards_of in cuts:
        steps = jax.random.uniform(jax.random.fold_in(jax.random.fold_in(stream_key, 6), axis_at), (shards_of,), jnp.float32, least / len(cuts), high / len(cuts))
        factor_of = factor_of * jnp.repeat(jnp.exp(steps), dims[axis_at] // shards_of).reshape((-1,) + (1,) * (len(dims) - 1 - axis_at))
    return factor_of


def gaussian(stream_key, extent, width, limit, split=(), kind=jnp.bfloat16):
    result = width * jax.random.normal(stream_key, extent, jnp.float32)
    if split:
        result = result * shard_levels(stream_key, extent, split, -0.22, 0.18)
    return jnp.clip(result, -limit, limit).astype(kind)


def setup_inputs(seed: int = 0) -> dict:
    key_of = jax.random.split(jax.random.key(seed), 7)
    return {
        "queries": draw_queries(jax.random.fold_in(key_of[6], 71), 0),
        "keys": draw_keys(jax.random.fold_in(key_of[6], 71), 0),
        "values": gaussian(key_of[2], (VIEWS, LEN, D), 1.0, 6.0, ((0, 8), (1, 32))),
        "hidden_in": gaussian(key_of[3], (VIEWS, LEN, D), 1.0, 6.0, ((0, 8), (1, 32))),
        "gate": jnp.clip(0.5 + 1.0 * jax.random.uniform(key_of[4], (VIEWS, D), jnp.float32) ** shard_levels(key_of[4], (VIEWS, D), ((0, 8),), -0.2, 0.2), 0.5, 1.5),
        "w_out": gaussian(key_of[5], (D, D), D ** -0.5, 0.15625),
    }


def attend(query, keyset, valueset):
    scores = jnp.dot(query, keyset.T, preferred_element_type=jnp.float32) * (HEAD_DIM ** -0.5)
    scores = scores - jnp.max(scores, axis=-1, keepdims=True)
    weights = jnp.exp(scores)
    weights = weights / jnp.sum(weights, axis=-1, keepdims=True)
    return jnp.dot(weights.astype(jnp.bfloat16), valueset, preferred_element_type=jnp.float32)


def pool_all(tensor):
    grouped = tensor.reshape(VIEWS, LEN // 4, 4, D).astype(jnp.float32)
    return jnp.mean(grouped, axis=2).astype(jnp.bfloat16)


def split_heads(rows):
    count = rows.shape[0]
    return rows.reshape(count, HEADS, HEAD_DIM).transpose(1, 0, 2)


def reference(queries, keys, values, hidden_in, gate, w_out):
    pooled_k = split_heads(pool_all(keys).reshape(VIEWS * (LEN // 4), D))
    pooled_v = split_heads(pool_all(values).reshape(VIEWS * (LEN // 4), D))

    def per_view(inputs):
        view_q, view_k, view_v, view_x, view_gate = inputs

        def per_head(head_inputs):
            head_q, head_k, head_v, cross_k, cross_v = head_inputs
            own = attend(head_q, head_k, head_v)
            other = attend(head_q, cross_k, cross_v)
            return (own + other).astype(jnp.bfloat16)

        heads_out = lax.map(per_head, (split_heads(view_q), split_heads(view_k), split_heads(view_v), pooled_k, pooled_v))
        rows_out = heads_out.transpose(1, 0, 2).reshape(LEN, D)
        projected = jnp.dot(rows_out, w_out, preferred_element_type=jnp.float32)
        return (view_x.astype(jnp.float32) + view_gate * projected).astype(jnp.bfloat16)

    return lax.map(per_view, (queries, keys, values, hidden_in, gate))
```

```python
import functools
import math

import jax
import jax.numpy as jnp
from jax import lax
from jax.experimental import pallas as pl
from jax.experimental.pallas import tpu as pltpu
from jax.sharding import Mesh, PartitionSpec as P

EXP2_SCALE = math.log2(math.e) / 8.0
VMEM = 56 * 2**20
AXES = ("y", "xh", "xl", "z", "core")
SIZES = (4, 2, 2, 8, 2)


def swap_halves(tile):
    return jnp.concatenate([tile[:, 64:], tile[:, :64]], axis=1)


def pair_heads(tile):
    half = tile.shape[0] // 2
    upper, lower = tile[:half], tile[half:]
    first = jnp.concatenate([upper[:, :64], lower[:, :64]], axis=1)
    second = jnp.concatenate([upper[:, 64:], lower[:, 64:]], axis=1)
    return first, second


def prep_kernel(q_ref, k_ref, v_ref, pool_ref, own_ref):
    rows = lax.broadcasted_iota(jnp.int32, (32, 128), 0)
    cols = lax.broadcasted_iota(jnp.int32, (32, 128), 1)
    mean4 = jnp.where(cols // 4 == rows, 0.25, 0.0).astype(jnp.bfloat16)
    for j in range(12):
        span = pl.ds(j * 128, 128)
        q, k, v = q_ref[:, span], k_ref[:, span], v_ref[:, span]
        qt, vt = q.T, v.T
        packed_k = pair_heads(k)
        pooled_k = pair_heads(
            jnp.dot(mean4, k, preferred_element_type=jnp.float32).astype(jnp.bfloat16)
        )
        pooled_v = pair_heads(
            jnp.dot(mean4, v, preferred_element_type=jnp.float32).astype(jnp.bfloat16)
        )
        for side in range(2):
            group, member = divmod(2 * j + side, 3)
            own_ref[group, 0, member] = qt[side * 64 : side * 64 + 64]
            own_ref[group, 1, member] = packed_k[side]
            own_ref[group, 2, member] = vt[side * 64 : side * 64 + 64]
            pool_ref[group, 0, member] = pooled_k[side]
            pool_ref[group, 1, member] = pooled_v[side]


def prep(q, k, v):
    return pl.pallas_call(
        prep_kernel,
        out_shape=(
            jax.ShapeDtypeStruct((8, 2, 3, 16, 128), jnp.bfloat16),
            jax.ShapeDtypeStruct((8, 3, 3, 64, 128), jnp.bfloat16),
        ),
        compiler_params=pltpu.CompilerParams(vmem_limit_bytes=VMEM),
        name="prep",
    )(q, k, v)


def repack_kernel(pool_ref, out_ref):
    for member in range(3):
        out_ref[member, 0] = pool_ref[:, 0, member].reshape(128, 128)
        out_ref[member, 1] = pool_ref[:, 1, member].reshape(128, 128).T


def repack(pool):
    return pl.pallas_call(
        repack_kernel,
        out_shape=jax.ShapeDtypeStruct((3, 2, 128, 128), jnp.bfloat16),
        name="repack",
    )(pool)


def own_tile(ref, tile):
    keys = ref[2 * tile : 2 * tile + 2, 0].reshape(128, 128)
    values = jnp.concatenate([ref[2 * tile, 1], ref[2 * tile + 1, 1]], axis=1)
    return keys, values


def own_order(p):
    return jnp.concatenate([p[0:64], p[128:192], p[64:128], p[192:256]], axis=0)


def pool_tile(ref, tile):
    both = ref[tile, 1]
    return ref[tile, 0], jnp.concatenate([both[:64], both[64:]], axis=1)


def pool_order(p):
    return p


def attend_kernel(count, tile_of, order, with_base, *refs):
    q_ref, kv_refs, rest = refs[0], refs[1 : 1 + count], refs[1 + count :]
    if with_base:
        base_ref, out_ref, s0, s1 = rest
    else:
        out_ref, s0, s1 = rest
    tiles = s0.shape[0]
    qt = jnp.concatenate([q_ref[0], q_ref[1]], axis=1)
    zero = jnp.zeros_like(qt)
    upper = jnp.concatenate([qt, zero], axis=0)
    lower = jnp.concatenate([zero, qt], axis=0)
    ones = jnp.ones((16, 256), jnp.bfloat16)

    def scores(ref, held):
        top = None
        for t in range(tiles):
            keys, _ = tile_of(ref, t)
            a = jnp.dot(keys, upper, preferred_element_type=jnp.float32)
            b = jnp.dot(keys, lower, preferred_element_type=jnp.float32)
            held[t, 0:128, :] = a
            held[t, 128:256, :] = b
            both = jnp.maximum(
                jnp.max(a.reshape(16, 8, 256), axis=0), jnp.max(b.reshape(16, 8, 256), axis=0)
            )
            top = both if top is None else jnp.maximum(top, both)
        return jnp.max(top, axis=0, keepdims=True)

    def weigh(ref, held, top, total):
        for t in range(tiles):
            _, values = tile_of(ref, t)
            p = jnp.exp2((held[t] - top) * EXP2_SCALE).astype(jnp.bfloat16)
            total = total + jnp.dot(
                jnp.concatenate([values, ones], axis=0),
                order(p),
                preferred_element_type=jnp.float32,
            )
        return total

    slots = (s0, s1)
    following = scores(kv_refs[0], s0)
    top, total = following, jnp.zeros((80, 256), jnp.float32)
    for b in range(count):
        newer = jnp.maximum(top, following)
        if b:
            total = total * jnp.exp2((top - newer) * EXP2_SCALE)
        top = newer
        if b + 1 < count:
            following = scores(kv_refs[b + 1], slots[(b + 1) % 2])
        total = weigh(kv_refs[b], slots[b % 2], top, total)
    result = total[0:64] / total[64:65]
    if with_base:
        result = (result + base_ref[...]).astype(jnp.bfloat16)
        out_ref[0] = result[:, :128]
        out_ref[1] = result[:, 128:]
    else:
        out_ref[...] = result


def attend(own, kvs, tile_of, order, tiles, base, name):
    count = len(kvs)
    in_specs = [pl.BlockSpec((2, None, None, 64, 128), lambda h, i: (i, 0, h, 0, 0))]
    for kv, at in kvs:
        shape = kv.shape
        if at == 2:
            in_specs.append(
                pl.BlockSpec((shape[0], shape[1], None, 64, 128), lambda h, i: (0, 0, h, 0, 0))
            )
        else:
            in_specs.append(
                pl.BlockSpec((shape[0], None, 2, 128, 128), lambda h, i: (0, h, 0, 0, 0))
            )
    args = [own] + [kv for kv, _ in kvs]
    if base is not None:
        args.append(base)
        in_specs.append(pl.BlockSpec((None, 64, 256), lambda h, i: (h, 0, i)))
        out_spec = pl.BlockSpec((2, None, 64, 128), lambda h, i: (i, h, 0, 0))
        out_shape = jax.ShapeDtypeStruct((8, 3, 64, 128), jnp.bfloat16)
    else:
        out_spec = pl.BlockSpec((None, 64, 256), lambda h, i: (h, 0, i))
        out_shape = jax.ShapeDtypeStruct((3, 64, 1024), jnp.float32)
    return pl.pallas_call(
        functools.partial(attend_kernel, count, tile_of, order, base is not None),
        grid=(3, 4),
        in_specs=in_specs,
        out_specs=out_spec,
        out_shape=out_shape,
        scratch_shapes=[pltpu.VMEM((tiles, 256, 256), jnp.float32)] * 2,
        compiler_params=pltpu.CompilerParams(vmem_limit_bytes=VMEM),
        name=name,
    )(*args)


def project_kernel(heads_ref, w_ref, hidden_ref, gate_ref, out_ref):
    projected = lax.dot_general(
        heads_ref[...], w_ref[...], (((0,), (0,)), ((), ())), preferred_element_type=jnp.float32
    )
    out_ref[...] = (hidden_ref[...].astype(jnp.float32) + gate_ref[...] * projected).astype(
        jnp.bfloat16
    )


def project(heads, w_out, hidden, gate):
    width = 512
    return pl.pallas_call(
        project_kernel,
        grid=(1536 // width,),
        in_specs=[
            pl.BlockSpec((1536, 128), lambda n: (0, 0)),
            pl.BlockSpec((1536, width), lambda n: (0, n)),
            pl.BlockSpec((128, width), lambda n: (0, n)),
            pl.BlockSpec((1, width), lambda n: (0, n)),
        ],
        out_specs=pl.BlockSpec((128, width), lambda n: (0, n)),
        out_shape=jax.ShapeDtypeStruct((128, 1536), jnp.bfloat16),
        compiler_params=pltpu.CompilerParams(vmem_limit_bytes=VMEM),
        name="project",
    )(heads, w_out, hidden, gate)


def shifted(array, axis, size, step):
    return lax.ppermute(array, axis, [(i, (i + step) % size) for i in range(size)])


def body(queries, keys, values, hidden_in, gate, w_out):
    pool, own = prep(queries[0], keys[0], values[0])
    pool = lax.all_to_all(pool, "z", 0, 0, tiled=True)
    own = lax.all_to_all(own, "z", 0, 0, tiled=True)
    piece = repack(pool)
    x = ("xh", "xl")
    row = jnp.stack([piece] + [shifted(piece, x, 4, step) for step in (1, 3, 2)])
    plane = [row] + [shifted(row, "y", 4, step) for step in (1, 3, 2)]
    crossed = plane + [shifted(part, "core", 2, 1) for part in plane]
    kv = own[:, 1:]
    kv_x = shifted(kv, "xl", 2, 1)
    column = [kv, shifted(kv, "core", 2, 1), kv_x, shifted(kv_x, "core", 2, 1)]
    base = attend(own, [(part, 2) for part in column], own_tile, own_order, 4, None, "own")
    heads = attend(own, [(part, 1) for part in crossed], pool_tile, pool_order, 4, base, "cross")
    returned = lax.all_to_all(heads, "z", 0, 0, tiled=True)
    result = project(returned.reshape(1536, 128), w_out, hidden_in[0], gate)
    return result[None]


def solution(mesh):
    fine = Mesh(mesh.devices.reshape(SIZES), AXES)
    tokens = P(("y", "xh"), ("xl", "z", "core"), None)
    placed = (tokens, tokens, tokens, tokens, P(("y", "xh"), None), P())
    return jax.shard_map(body, mesh=fine, in_specs=placed, out_specs=tokens, check_vma=False)
```

```python
import functools
import math

import jax
import jax.numpy as jnp
from jax import lax
from jax.experimental import pallas as pl
from jax.experimental.pallas import tpu as pltpu
from jax.sharding import Mesh, PartitionSpec as P

EXP2_SCALE = math.log2(math.e) / 8.0
VMEM = 32 * 2**20
PREP_PARAMS = pltpu.CompilerParams(vmem_limit_bytes=60 * 2**20)
PARAMS = pltpu.CompilerParams(vmem_limit_bytes=VMEM)
LEAST, MOST = 2.0**-64, 2.0**64
AXES = ("y", "xh", "xl", "z", "core")
SIZES = (4, 2, 2, 8, 2)


def swap_halves(tile):
    return jnp.concatenate([tile[:, 64:], tile[:, :64]], axis=1)


def pair_heads(tile):
    half = tile.shape[0] // 2
    upper, lower = tile[:half], tile[half:]
    first = jnp.concatenate([upper[:, :64], lower[:, :64]], axis=1)
    second = jnp.concatenate([upper[:, 64:], lower[:, 64:]], axis=1)
    return first, second


def prep_kernel(q_ref, k_ref, v_ref, pool_ref, own_ref):
    rows = lax.broadcasted_iota(jnp.int32, (32, 128), 0)
    cols = lax.broadcasted_iota(jnp.int32, (32, 128), 1)
    mean4 = jnp.where(cols // 4 == rows, 0.25, 0.0).astype(jnp.bfloat16)
    for j in range(12):
        span = pl.ds(j * 128, 128)
        q, k, v = q_ref[:, span], k_ref[:, span], v_ref[:, span]
        qt, vt = q.T, v.T
        packed_k = pair_heads(k)
        pooled_k = pair_heads(
            jnp.dot(mean4, k, preferred_element_type=jnp.float32).astype(jnp.bfloat16)
        )
        pooled_v = pair_heads(
            jnp.dot(mean4, v, preferred_element_type=jnp.float32).astype(jnp.bfloat16)
        )
        for side in range(2):
            group, member = divmod(2 * j + side, 3)
            own_ref[group, member, 0:64] = qt[side * 64 : side * 64 + 64]
            own_ref[group, member, 64:128] = packed_k[side]
            own_ref[group, member, 128:192] = vt[side * 64 : side * 64 + 64]
            pool_ref[group, 0, member] = pooled_k[side]
            pool_ref[group, 1, member] = pooled_v[side]


def prep(q, k, v):
    return pl.pallas_call(
        prep_kernel,
        out_shape=(
            jax.ShapeDtypeStruct((8, 2, 3, 16, 128), jnp.bfloat16),
            jax.ShapeDtypeStruct((8, 3, 192, 128), jnp.bfloat16),
        ),
        compiler_params=PREP_PARAMS,
        name="prep",
    )(q, k, v)


def repack_kernel(pool_ref, out_ref):
    for member in range(3):
        out_ref[0, member] = pool_ref[:, 0, member].reshape(128, 128)
        out_ref[1, member] = pool_ref[:, 1, member].reshape(128, 128).T


def repack(pool):
    return pl.pallas_call(
        repack_kernel,
        out_shape=jax.ShapeDtypeStruct((2, 3, 128, 128), jnp.bfloat16),
        name="repack",
    )(pool)


def both_places(qt):
    zero = jnp.zeros_like(qt)
    return jnp.concatenate([qt, zero], axis=0), jnp.concatenate([zero, qt], axis=0)


def score(keys, queries):
    return jnp.dot(keys, queries, preferred_element_type=jnp.float32)


def outside(totals):
    return jnp.logical_not((jnp.min(totals) > LEAST) & (jnp.max(totals) < MOST))


def peak(a):
    return jnp.max(a.reshape(-1, 8, a.shape[1]), axis=0)


def joined(near, far):
    most = jnp.maximum(near[72:73], far[72:73])
    near_by = jnp.exp2((near[72:73] - most) * EXP2_SCALE)
    far_by = jnp.exp2((far[72:73] - most) * EXP2_SCALE)
    return near[0:72] * near_by + far[0:72] * far_by, most


def row_keys(row, head):
    return row[0, :, head].reshape(512, 128)


def row_weighted(row, head, p):
    parts = [row[1, x, head] for x in range(4)]
    values = jnp.concatenate([v[:64] for v in parts] + [v[64:] for v in parts], axis=1)
    ones = jnp.ones((16, 1024), jnp.bfloat16)
    return score(jnp.concatenate([values, ones], axis=0), p)


def cross_head(head, q_ref, rows, out_ref):
    upper, lower = both_places(jnp.concatenate([q_ref[z, head] for z in range(8)], axis=1))
    total = jnp.zeros((80, 1024), jnp.float32)
    for row in rows:
        p = [
            jnp.exp2(score(row_keys(row, head), place) * EXP2_SCALE).astype(jnp.bfloat16)
            for place in (upper, lower)
        ]
        total = total + row_weighted(row, head, jnp.concatenate(p, axis=0))
    out_ref[head, 0:72] = total[0:72]
    out_ref[head, 72:80] = jnp.zeros((8, 1024), jnp.float32)


def cross_shifted(head, q_ref, rows, out_ref):
    def one(i, carry):
        places = both_places(jnp.concatenate([q_ref[2 * i, head], q_ref[2 * i + 1, head]], axis=1))
        top = jnp.full((1, 256), -jnp.inf, jnp.float32)
        total = jnp.zeros((80, 256), jnp.float32)
        for row in rows:
            a = jnp.concatenate([score(row_keys(row, head), place) for place in places], axis=0)
            newer = jnp.maximum(top, jnp.max(peak(a), axis=0, keepdims=True))
            p = jnp.exp2((a - newer) * EXP2_SCALE).astype(jnp.bfloat16)
            total = total * jnp.exp2((top - newer) * EXP2_SCALE) + row_weighted(row, head, p)
            top = newer
        span = pl.ds(pl.multiple_of(i * 256, 256), 256)
        out_ref[head, 0:72, span] = total[0:72]
        out_ref[head, 72:80, span] = jnp.broadcast_to(top, (8, 256))
        return carry

    lax.fori_loop(0, 4, one, 0)


def each_head(count, step, unroll=False):
    if unroll:
        for head in range(count):
            step(head)
    else:
        lax.fori_loop(0, count, lambda head, carry: (step(head), carry)[1], 0)


def cross_kernel(sides, count, *refs):
    q_refs, rows, rest = refs[:sides], refs[sides : sides + count], refs[sides + count :]
    before_refs, out_refs = rest[:-sides], rest[-sides:]

    def plain(head):
        for side in range(sides):
            cross_head(head, q_refs[side], rows, out_refs[side])

    each_head(3, plain, unroll=True)
    totals = jnp.concatenate([ref[:, 64:65] for ref in out_refs], axis=0)

    @pl.when(outside(totals))
    def _():
        for side in range(sides):
            each_head(3, lambda head: cross_shifted(head, q_refs[side], rows, out_refs[side]))

    def join(head):
        for before_ref, out_ref in zip(before_refs, out_refs):
            whole, most = joined(out_ref[head], before_ref[head])
            out_ref[head, 0:72] = whole
            out_ref[head, 72:80] = jnp.broadcast_to(most, (8, 1024))

    if before_refs:
        each_head(3, join)


def own_keys(kvs, head, block):
    return kvs[block][:, head, 0:64].reshape(512, 128)


def own_values(kvs, head, block):
    return jnp.concatenate([kvs[block][c, head, 64:128] for c in range(8)], axis=1)


def own_finish(head, kvs, near_ref, far_ref, out_ref, p_ref, sums):
    by = 1.0 / sums
    total = jnp.zeros((64, 1024), jnp.float32)
    for block in range(4):
        w = (p_ref[8 * block : 8 * block + 8].reshape(1024, 1024) * by).astype(jnp.bfloat16)
        total = total + score(own_values(kvs, head, block), w)
    whole, _ = joined(near_ref[head], far_ref[head])
    result = (total + whole[0:64] / whole[64:65]).astype(jnp.bfloat16)
    for z in range(8):
        out_ref[z, head] = result[:, 128 * z : 128 * z + 128]


def own_weights(head, q_ref, kvs, p_ref):
    upper, lower = both_places(jnp.concatenate([q_ref[z, head] for z in range(8)], axis=1))
    sums = jnp.zeros((8, 1024), jnp.float32)
    for block in range(4):
        for side, place in enumerate((upper, lower)):
            p = jnp.exp2(score(own_keys(kvs, head, block), place) * EXP2_SCALE)
            p_ref[8 * block : 8 * block + 8, 64 * side : 64 * side + 64] = p.reshape(8, 64, 1024)
            sums = sums + jnp.sum(p.reshape(-1, 8, 1024), axis=0)
    return jnp.sum(sums, axis=0, keepdims=True)


def own_shifted(head, q_ref, kvs, p_ref, sum_ref):
    def one(i, carry):
        span = pl.ds(pl.multiple_of(i * 256, 256), 256)
        places = both_places(jnp.concatenate([q_ref[2 * i, head], q_ref[2 * i + 1, head]], axis=1))
        top = jnp.full((8, 256), -jnp.inf, jnp.float32)
        for block in range(4):
            for side, place in enumerate(places):
                a = score(own_keys(kvs, head, block), place)
                p_ref[8 * block : 8 * block + 8, 64 * side : 64 * side + 64, span] = a.reshape(
                    8, 64, 256
                )
                top = jnp.maximum(top, peak(a))
        top = jnp.max(top, axis=0, keepdims=True)
        sums = jnp.zeros((8, 256), jnp.float32)
        for block in range(4):
            p = jnp.exp2((p_ref[8 * block : 8 * block + 8, :, span] - top) * EXP2_SCALE)
            p_ref[8 * block : 8 * block + 8, :, span] = p
            sums = sums + jnp.sum(p.reshape(-1, 8, 256), axis=0)
        sum_ref[head, 0:1, span] = jnp.sum(sums, axis=0, keepdims=True)
        return carry

    lax.fori_loop(0, 4, one, 0)


def own_kernel(q_ref, kv0, kv1, kv2, kv3, near_ref, far_ref, out_ref, p_ref, sum_ref):
    kvs = (kv0, kv1, kv2, kv3)
    rest = kvs, near_ref, far_ref, out_ref, p_ref

    def plain(head):
        sums = own_weights(head, q_ref, kvs, p_ref)
        sum_ref[head, 0:1] = sums
        own_finish(head, *rest, sums)

    each_head(3, plain)

    @pl.when(outside(sum_ref[:, 0:1]))
    def _():
        def again(head):
            own_shifted(head, q_ref, kvs, p_ref, sum_ref)
            own_finish(head, *rest, sum_ref[head, 0:1])

        each_head(3, again)


def cross_attend(queries, rows, before):
    sides = len(queries)
    sums = jax.ShapeDtypeStruct((3, 80, 1024), jnp.float32)
    return pl.pallas_call(
        functools.partial(cross_kernel, sides, len(rows)),
        out_shape=[sums] * sides,
        compiler_params=PARAMS,
        name="cross",
    )(*queries, *rows, *before)


def own_attend(q, column, near, far):
    return pl.pallas_call(
        own_kernel,
        out_shape=jax.ShapeDtypeStruct((8, 3, 64, 128), jnp.bfloat16),
        scratch_shapes=[
            pltpu.VMEM((32, 128, 1024), jnp.float32),
            pltpu.VMEM((3, 8, 1024), jnp.float32),
        ],
        compiler_params=PARAMS,
        name="own",
    )(q, *column, near, far)


def project_kernel(heads_ref, w_ref, hidden_ref, gate_ref, out_ref):
    rows = jnp.concatenate(
        [heads_ref[128 * j : 128 * j + 128].T for j in range(12)], axis=1
    )
    projected = jnp.dot(rows, w_ref[...], preferred_element_type=jnp.float32)
    out_ref[...] = (hidden_ref[...].astype(jnp.float32) + gate_ref[...] * projected).astype(
        jnp.bfloat16
    )


def project(heads, w_out, hidden, gate):
    return pl.pallas_call(
        project_kernel,
        out_shape=jax.ShapeDtypeStruct((128, 1536), jnp.bfloat16),
        compiler_params=PARAMS,
        name="project",
    )(heads, w_out, hidden, gate)


def shifted(array, axis, size, step):
    return lax.ppermute(array, axis, [(i, (i + step) % size) for i in range(size)])


def body(queries, keys, values, hidden_in, gate, w_out):
    x, y = ("xh", "xl"), "y"
    pool, own = prep(queries[0], keys[0], values[0])
    pool = lax.all_to_all(pool, "z", 0, 0, tiled=True)
    own = lax.all_to_all(own, "z", 0, 0, tiled=True)
    piece = repack(pool)
    row = jnp.stack([piece] + [shifted(piece, x, 4, step) for step in (1, 3, 2)], axis=1)
    back, ahead = shifted(row, y, 4, 1), shifted(row, y, 4, 3)
    across = shifted(back, y, 4, 1)
    q, kv = own[:, :, :64], own[:, :, 64:]
    kv_x = shifted(kv, "xl", 2, 1)
    column = [kv, shifted(kv, "core", 2, 1), kv_x, shifted(kv_x, "core", 2, 1)]
    q_far = shifted(q, "core", 2, 1)
    sums = cross_attend([q_far, q], [row], [])
    sums = cross_attend([q_far, q], [back, ahead], sums)
    (far,) = cross_attend([q_far], [across], sums[:1])
    far = shifted(far, "core", 2, 1)
    (near,) = cross_attend([q], [across], sums[1:])
    heads = own_attend(q, column, near, far)
    returned = lax.all_to_all(heads, "z", 0, 0, tiled=True)
    result = project(returned.reshape(1536, 128), w_out, hidden_in[0], gate)
    return result[None]


def solution(mesh):
    fine = Mesh(mesh.devices.reshape(SIZES), AXES)
    tokens = P(("y", "xh"), ("xl", "z", "core"), None)
    placed = (tokens, tokens, tokens, tokens, P(("y", "xh"), None), P())
    return jax.shard_map(body, mesh=fine, in_specs=placed, out_specs=tokens, check_vma=False)
```

```python
import functools
import math

import jax
import jax.numpy as jnp
from jax import lax
from jax.experimental import pallas as pl
from jax.experimental.pallas import tpu as pltpu
from jax.sharding import Mesh, PartitionSpec as P

EXP2_SCALE = math.log2(math.e) / 8.0
VMEM = 32 * 2**20
PREP_PARAMS = pltpu.CompilerParams(vmem_limit_bytes=60 * 2**20)
PARAMS = pltpu.CompilerParams(vmem_limit_bytes=VMEM)
LEAST, MOST = 2.0**-64, 2.0**64
AXES = ("y", "xh", "xl", "z", "core")
SIZES = (4, 2, 2, 8, 2)


def swap_halves(tile):
    return jnp.concatenate([tile[:, 64:], tile[:, :64]], axis=1)


def pair_heads(tile):
    half = tile.shape[0] // 2
    upper, lower = tile[:half], tile[half:]
    first = jnp.concatenate([upper[:, :64], lower[:, :64]], axis=1)
    second = jnp.concatenate([upper[:, 64:], lower[:, 64:]], axis=1)
    return first, second


def prep_kernel(q_ref, k_ref, v_ref, pool_ref, own_ref):
    rows = lax.broadcasted_iota(jnp.int32, (32, 128), 0)
    cols = lax.broadcasted_iota(jnp.int32, (32, 128), 1)
    mean4 = jnp.where(cols // 4 == rows, 0.25, 0.0).astype(jnp.bfloat16)
    for j in range(12):
        span = pl.ds(j * 128, 128)
        q, k, v = q_ref[:, span], k_ref[:, span], v_ref[:, span]
        qt, vt = q.T, v.T
        packed_k = pair_heads(k)
        pooled_k = pair_heads(
            jnp.dot(mean4, k, preferred_element_type=jnp.float32).astype(jnp.bfloat16)
        )
        pooled_v = pair_heads(
            jnp.dot(mean4, v, preferred_element_type=jnp.float32).astype(jnp.bfloat16)
        )
        for side in range(2):
            group, member = divmod(2 * j + side, 3)
            own_ref[group, member, 0:64] = qt[side * 64 : side * 64 + 64]
            own_ref[group, member, 64:128] = packed_k[side]
            own_ref[group, member, 128:192] = vt[side * 64 : side * 64 + 64]
            pool_ref[group, 0, member] = pooled_k[side]
            pool_ref[group, 1, member] = pooled_v[side]


def prep(q, k, v):
    return pl.pallas_call(
        prep_kernel,
        out_shape=(
            jax.ShapeDtypeStruct((8, 2, 3, 16, 128), jnp.bfloat16),
            jax.ShapeDtypeStruct((8, 3, 192, 128), jnp.bfloat16),
        ),
        compiler_params=PREP_PARAMS,
        name="prep",
    )(q, k, v)


def repack_kernel(pool_ref, out_ref):
    for member in range(3):
        out_ref[0, member] = pool_ref[:, 0, member].reshape(128, 128)
        out_ref[1, member] = pool_ref[:, 1, member].reshape(128, 128).T


def repack(pool):
    return pl.pallas_call(
        repack_kernel,
        out_shape=jax.ShapeDtypeStruct((2, 3, 128, 128), jnp.bfloat16),
        name="repack",
    )(pool)


def both_places(qt):
    zero = jnp.zeros_like(qt)
    return jnp.concatenate([qt, zero], axis=0), jnp.concatenate([zero, qt], axis=0)


def score(keys, queries):
    return jnp.dot(keys, queries, preferred_element_type=jnp.float32)


def outside(totals):
    return jnp.logical_not((jnp.min(totals) > LEAST) & (jnp.max(totals) < MOST))


def peak(a):
    return jnp.max(a.reshape(-1, 8, a.shape[1]), axis=0)


def joined(near, far):
    most = jnp.maximum(near[72:73], far[72:73])
    near_by = jnp.exp2((near[72:73] - most) * EXP2_SCALE)
    far_by = jnp.exp2((far[72:73] - most) * EXP2_SCALE)
    return near[0:72] * near_by + far[0:72] * far_by, most


def row_keys(row, head):
    return row[0, :, head].reshape(512, 128)


def row_weighted(row, head, p):
    parts = [row[1, x, head] for x in range(4)]
    values = jnp.concatenate([v[:64] for v in parts] + [v[64:] for v in parts], axis=1)
    ones = jnp.ones((16, 1024), jnp.bfloat16)
    return score(jnp.concatenate([values, ones], axis=0), p)


def cross_head(head, q_ref, rows, out_ref):
    upper, lower = both_places(jnp.concatenate([q_ref[z, head] for z in range(8)], axis=1))
    total = jnp.zeros((80, 1024), jnp.float32)
    for row in rows:
        p = [
            jnp.exp2(score(row_keys(row, head), place) * EXP2_SCALE).astype(jnp.bfloat16)
            for place in (upper, lower)
        ]
        total = total + row_weighted(row, head, jnp.concatenate(p, axis=0))
    out_ref[head, 0:72] = total[0:72]
    out_ref[head, 72:80] = jnp.zeros((8, 1024), jnp.float32)


def cross_shifted(head, q_ref, rows, out_ref):
    def one(i, carry):
        places = both_places(jnp.concatenate([q_ref[2 * i, head], q_ref[2 * i + 1, head]], axis=1))
        span = pl.ds(pl.multiple_of(i * 256, 256), 256)
        ones = jnp.ones((16, 256), jnp.bfloat16)
        out_ref[head, 0:72, span] = jnp.zeros((72, 256), jnp.float32)
        out_ref[head, 72:80, span] = jnp.full((8, 256), -jnp.inf, jnp.float32)
        for row in rows:

            def some(x, carry):
                a = jnp.concatenate([score(row[0, x, head], place) for place in places], axis=0)
                top = out_ref[head, 72:73, span]
                newer = jnp.maximum(top, jnp.max(peak(a), axis=0, keepdims=True))
                p = jnp.exp2((a - newer) * EXP2_SCALE).astype(jnp.bfloat16)
                v = row[1, x, head]
                values = jnp.concatenate([jnp.concatenate([v[:64], v[64:]], axis=1), ones], axis=0)
                total = out_ref[head, 0:72, span] * jnp.exp2((top - newer) * EXP2_SCALE)
                out_ref[head, 0:72, span] = total + score(values, p)[0:72]
                out_ref[head, 72:80, span] = jnp.broadcast_to(newer, (8, 256))
                return carry

            lax.fori_loop(0, 4, some, 0)
        return carry

    lax.fori_loop(0, 4, one, 0)


def each_head(count, step, unroll=False):
    if unroll:
        for head in range(count):
            step(head)
    else:
        lax.fori_loop(0, count, lambda head, carry: (step(head), carry)[1], 0)


def cross_kernel(sides, count, *refs):
    q_refs, rows, rest = refs[:sides], refs[sides : sides + count], refs[sides + count :]
    before_refs, out_refs = rest[:-sides], rest[-sides:]

    def plain(head):
        for side in range(sides):
            cross_head(head, q_refs[side], rows, out_refs[side])

    each_head(3, plain)
    totals = jnp.concatenate([ref[:, 64:65] for ref in out_refs], axis=0)

    @pl.when(outside(totals))
    def _():
        for side in range(sides):
            each_head(3, lambda head: cross_shifted(head, q_refs[side], rows, out_refs[side]))

    def join(head):
        for before_ref, out_ref in zip(before_refs, out_refs):
            whole, most = joined(out_ref[head], before_ref[head])
            out_ref[head, 0:72] = whole
            out_ref[head, 72:80] = jnp.broadcast_to(most, (8, 1024))

    if before_refs:
        each_head(3, join)


def own_keys(kvs, head, block):
    return kvs[block][:, head, 0:64].reshape(512, 128)


def own_values(kvs, head, block):
    return jnp.concatenate([kvs[block][c, head, 64:128] for c in range(8)], axis=1)


def own_finish(head, kvs, near_ref, far_ref, out_ref, p_ref, sums):
    by = 1.0 / sums
    total = jnp.zeros((64, 1024), jnp.float32)
    for block in range(4):
        w = (p_ref[8 * block : 8 * block + 8].reshape(1024, 1024) * by).astype(jnp.bfloat16)
        total = total + score(own_values(kvs, head, block), w)
    whole, _ = joined(near_ref[head], far_ref[head])
    result = (total + whole[0:64] / whole[64:65]).astype(jnp.bfloat16)
    for z in range(8):
        out_ref[z, head] = result[:, 128 * z : 128 * z + 128]


def own_weights(head, q_ref, kvs, p_ref):
    upper, lower = both_places(jnp.concatenate([q_ref[z, head] for z in range(8)], axis=1))
    sums = jnp.zeros((8, 1024), jnp.float32)
    for block in range(4):
        for side, place in enumerate((upper, lower)):
            p = jnp.exp2(score(own_keys(kvs, head, block), place) * EXP2_SCALE)
            p_ref[8 * block : 8 * block + 8, 64 * side : 64 * side + 64] = p.reshape(8, 64, 1024)
            sums = sums + jnp.sum(p.reshape(-1, 8, 1024), axis=0)
    return jnp.sum(sums, axis=0, keepdims=True)


def own_shifted(head, q_ref, kvs, p_ref, sum_ref):
    def one(i, carry):
        span = pl.ds(pl.multiple_of(i * 256, 256), 256)
        places = both_places(jnp.concatenate([q_ref[2 * i, head], q_ref[2 * i + 1, head]], axis=1))
        top = jnp.full((8, 256), -jnp.inf, jnp.float32)
        for block, kv in enumerate(kvs):

            def scored(c, top):
                for side, place in enumerate(places):
                    a = score(kv[c, head, 0:64], place)
                    p_ref[8 * block + c, 64 * side : 64 * side + 64, span] = a
                    top = jnp.maximum(top, peak(a))
                return top

            top = lax.fori_loop(0, 8, scored, top)
        top = jnp.max(top, axis=0, keepdims=True)

        def weighed(c, sums):
            p = jnp.exp2((p_ref[c, :, span] - top) * EXP2_SCALE)
            p_ref[c, :, span] = p
            return sums + jnp.sum(p.reshape(16, 8, 256), axis=0)

        sums = lax.fori_loop(0, 32, weighed, jnp.zeros((8, 256), jnp.float32))
        sum_ref[head, 0:1, span] = jnp.sum(sums, axis=0, keepdims=True)
        return carry

    lax.fori_loop(0, 4, one, 0)


def own_kernel(q_ref, kv0, kv1, kv2, kv3, near_ref, far_ref, out_ref, p_ref, sum_ref):
    kvs = (kv0, kv1, kv2, kv3)
    rest = kvs, near_ref, far_ref, out_ref, p_ref

    def whole(head):
        sum_ref[head, 0:1] = own_weights(head, q_ref, kvs, p_ref)

        @pl.when(outside(sum_ref[head, 0:1]))
        def _():
            own_shifted(head, q_ref, kvs, p_ref, sum_ref)

        own_finish(head, *rest, sum_ref[head, 0:1])

    each_head(3, whole)


def cross_attend(queries, rows, before):
    sides = len(queries)
    sums = jax.ShapeDtypeStruct((3, 80, 1024), jnp.float32)
    return pl.pallas_call(
        functools.partial(cross_kernel, sides, len(rows)),
        out_shape=[sums] * sides,
        compiler_params=PARAMS,
        name="cross",
    )(*queries, *rows, *before)


def own_attend(q, column, near, far):
    return pl.pallas_call(
        own_kernel,
        out_shape=jax.ShapeDtypeStruct((8, 3, 64, 128), jnp.bfloat16),
        scratch_shapes=[
            pltpu.VMEM((32, 128, 1024), jnp.float32),
            pltpu.VMEM((3, 8, 1024), jnp.float32),
        ],
        compiler_params=PARAMS,
        name="own",
    )(q, *column, near, far)


def project_kernel(heads_ref, w_ref, hidden_ref, gate_ref, out_ref):
    rows = jnp.concatenate(
        [heads_ref[128 * j : 128 * j + 128].T for j in range(12)], axis=1
    )
    projected = jnp.dot(rows, w_ref[...], preferred_element_type=jnp.float32)
    out_ref[...] = (hidden_ref[...].astype(jnp.float32) + gate_ref[...] * projected).astype(
        jnp.bfloat16
    )


def project(heads, w_out, hidden, gate):
    return pl.pallas_call(
        project_kernel,
        out_shape=jax.ShapeDtypeStruct((128, 1536), jnp.bfloat16),
        compiler_params=PARAMS,
        name="project",
    )(heads, w_out, hidden, gate)


def shifted(array, axis, size, step):
    return lax.ppermute(array, axis, [(i, (i + step) % size) for i in range(size)])


def body(queries, keys, values, hidden_in, gate, w_out):
    x, y = ("xh", "xl"), "y"
    pool, own = prep(queries[0], keys[0], values[0])
    pool = lax.all_to_all(pool, "z", 0, 0, tiled=True)
    own = lax.all_to_all(own, "z", 0, 0, tiled=True)
    piece = repack(pool)
    row = jnp.stack([piece] + [shifted(piece, x, 4, step) for step in (1, 3, 2)], axis=1)
    back, ahead = shifted(row, y, 4, 1), shifted(row, y, 4, 3)
    across = shifted(back, y, 4, 1)
    q, kv = own[:, :, :64], own[:, :, 64:]
    kv_x = shifted(kv, "xl", 2, 1)
    column = [kv, shifted(kv, "core", 2, 1), kv_x, shifted(kv_x, "core", 2, 1)]
    q_far = shifted(q, "core", 2, 1)
    sums = cross_attend([q_far, q], [row], [])
    sums = cross_attend([q_far, q], [back, ahead], sums)
    (far,) = cross_attend([q_far], [across], sums[:1])
    far = shifted(far, "core", 2, 1)
    (near,) = cross_attend([q], [across], sums[1:])
    heads = own_attend(q, column, near, far)
    returned = lax.all_to_all(heads, "z", 0, 0, tiled=True)
    result = project(returned.reshape(1536, 128), w_out, hidden_in[0], gate)
    return result[None]


def solution(mesh):
    fine = Mesh(mesh.devices.reshape(SIZES), AXES)
    tokens = P(("y", "xh"), ("xl", "z", "core"), None)
    placed = (tokens, tokens, tokens, tokens, P(("y", "xh"), None), P())
    return jax.shard_map(body, mesh=fine, in_specs=placed, out_specs=tokens, check_vma=False)
```

```python
import functools
import math

import jax
import jax.numpy as jnp
from jax import lax
from jax.experimental import pallas as pl
from jax.experimental.pallas import tpu as pltpu
from jax.sharding import Mesh, PartitionSpec as P

EXP2_SCALE = math.log2(math.e) / 8.0
VMEM = 20 * 2**20
OWN_PARAMS = pltpu.CompilerParams(vmem_limit_bytes=32 * 2**20)
PREP_PARAMS = pltpu.CompilerParams(vmem_limit_bytes=60 * 2**20)
PARAMS = pltpu.CompilerParams(vmem_limit_bytes=VMEM)
LEAST, MOST = 2.0**-64, 2.0**64
AXES = ("y", "xh", "xl", "z", "core")
SIZES = (4, 2, 2, 8, 2)


def swap_halves(tile):
    return jnp.concatenate([tile[:, 64:], tile[:, :64]], axis=1)


def pair_heads(tile):
    half = tile.shape[0] // 2
    upper, lower = tile[:half], tile[half:]
    first = jnp.concatenate([upper[:, :64], lower[:, :64]], axis=1)
    second = jnp.concatenate([upper[:, 64:], lower[:, 64:]], axis=1)
    return first, second


def prep_kernel(q_ref, k_ref, v_ref, pool_ref, own_ref):
    rows = lax.broadcasted_iota(jnp.int32, (32, 128), 0)
    cols = lax.broadcasted_iota(jnp.int32, (32, 128), 1)
    mean4 = jnp.where(cols // 4 == rows, 0.25, 0.0).astype(jnp.bfloat16)
    for j in range(12):
        span = pl.ds(j * 128, 128)
        q, k, v = q_ref[:, span], k_ref[:, span], v_ref[:, span]
        qt, vt = q.T, v.T
        packed_k = pair_heads(k)
        pooled_k = pair_heads(
            jnp.dot(mean4, k, preferred_element_type=jnp.float32).astype(jnp.bfloat16)
        )
        pooled_v = pair_heads(
            jnp.dot(mean4, v, preferred_element_type=jnp.float32).astype(jnp.bfloat16)
        )
        for side in range(2):
            group, member = divmod(2 * j + side, 3)
            own_ref[group, member, 0:64] = qt[side * 64 : side * 64 + 64]
            own_ref[group, member, 64:128] = packed_k[side]
            own_ref[group, member, 128:192] = vt[side * 64 : side * 64 + 64]
            pool_ref[group, 0, member] = pooled_k[side]
            pool_ref[group, 1, member] = pooled_v[side]


def prep(q, k, v):
    return pl.pallas_call(
        prep_kernel,
        out_shape=(
            jax.ShapeDtypeStruct((8, 2, 3, 16, 128), jnp.bfloat16),
            jax.ShapeDtypeStruct((8, 3, 192, 128), jnp.bfloat16),
        ),
        compiler_params=PREP_PARAMS,
        name="prep",
    )(q, k, v)


def repack_kernel(pool_ref, out_ref):
    for member in range(3):
        out_ref[0, member] = pool_ref[:, 0, member].reshape(128, 128)
        out_ref[1, member] = pool_ref[:, 1, member].reshape(128, 128).T


def repack(pool):
    return pl.pallas_call(
        repack_kernel,
        out_shape=jax.ShapeDtypeStruct((2, 3, 128, 128), jnp.bfloat16),
        compiler_params=PARAMS,
        name="repack",
    )(pool)


def both_places(qt):
    zero = jnp.zeros_like(qt)
    return jnp.concatenate([qt, zero], axis=0), jnp.concatenate([zero, qt], axis=0)


def score(keys, queries):
    return jnp.dot(keys, queries, preferred_element_type=jnp.float32)


def outside(totals):
    return jnp.logical_not((jnp.min(totals) > LEAST) & (jnp.max(totals) < MOST))


def peak(a):
    return jnp.max(a.reshape(-1, 8, a.shape[1]), axis=0)


def joined(near, far):
    most = jnp.maximum(near[72:73], far[72:73])
    near_by = jnp.exp2((near[72:73] - most) * EXP2_SCALE)
    far_by = jnp.exp2((far[72:73] - most) * EXP2_SCALE)
    return near[0:72] * near_by + far[0:72] * far_by, most


def row_keys(row, head):
    return row[0, :, head].reshape(512, 128)


def row_weighted(row, head, p):
    parts = [row[1, x, head] for x in range(4)]
    values = jnp.concatenate([v[:64] for v in parts] + [v[64:] for v in parts], axis=1)
    ones = jnp.ones((16, 1024), jnp.bfloat16)
    return score(jnp.concatenate([values, ones], axis=0), p)


def cross_head(head, q_ref, rows, out_ref):
    upper, lower = both_places(jnp.concatenate([q_ref[z, head] for z in range(8)], axis=1))
    total = jnp.zeros((80, 1024), jnp.float32)
    for row in rows:
        p = [
            jnp.exp2(score(row_keys(row, head), place) * EXP2_SCALE).astype(jnp.bfloat16)
            for place in (upper, lower)
        ]
        total = total + row_weighted(row, head, jnp.concatenate(p, axis=0))
    out_ref[head, 0:72] = total[0:72]
    out_ref[head, 72:80] = jnp.zeros((8, 1024), jnp.float32)


def cross_shifted(head, q_ref, rows, out_ref):
    def one(i, carry):
        places = both_places(jnp.concatenate([q_ref[2 * i, head], q_ref[2 * i + 1, head]], axis=1))
        span = pl.ds(pl.multiple_of(i * 256, 256), 256)
        ones = jnp.ones((16, 256), jnp.bfloat16)
        out_ref[head, 0:72, span] = jnp.zeros((72, 256), jnp.float32)
        out_ref[head, 72:80, span] = jnp.full((8, 256), -jnp.inf, jnp.float32)
        for row in rows:

            def some(x, carry):
                a = jnp.concatenate([score(row[0, x, head], place) for place in places], axis=0)
                top = out_ref[head, 72:73, span]
                newer = jnp.maximum(top, jnp.max(peak(a), axis=0, keepdims=True))
                p = jnp.exp2((a - newer) * EXP2_SCALE).astype(jnp.bfloat16)
                v = row[1, x, head]
                values = jnp.concatenate([jnp.concatenate([v[:64], v[64:]], axis=1), ones], axis=0)
                total = out_ref[head, 0:72, span] * jnp.exp2((top - newer) * EXP2_SCALE)
                out_ref[head, 0:72, span] = total + score(values, p)[0:72]
                out_ref[head, 72:80, span] = jnp.broadcast_to(newer, (8, 256))
                return carry

            lax.fori_loop(0, 4, some, 0)
        return carry

    lax.fori_loop(0, 4, one, 0)


def each_head(count, step, unroll=False):
    if unroll:
        for head in range(count):
            step(head)
    else:
        lax.fori_loop(0, count, lambda head, carry: (step(head), carry)[1], 0)


def cross_kernel(count, has_before, has_token, q_ref, *refs):
    rows, out_ref = refs[:count], refs[-1]
    if has_token:
        refs[-2][...] = jnp.zeros((8, 128), jnp.float32)
    each_head(3, lambda head: cross_head(head, q_ref, rows, out_ref))

    @pl.when(outside(out_ref[:, 64:65]))
    def _():
        each_head(3, lambda head: cross_shifted(head, q_ref, rows, out_ref))

    def join(head):
        whole, most = joined(out_ref[head], refs[count][head])
        out_ref[head, 0:72] = whole
        out_ref[head, 72:80] = jnp.broadcast_to(most, (8, 1024))

    if has_before:
        each_head(3, join)


def own_keys(kvs, head, block):
    return kvs[block][:, head, 0:64].reshape(512, 128)


def own_values(kvs, head, block):
    return jnp.concatenate([kvs[block][c, head, 64:128] for c in range(8)], axis=1)


def own_finish(head, kvs, near_ref, far_ref, out_ref, p_ref, sums):
    by = 1.0 / sums
    total = jnp.zeros((64, 1024), jnp.float32)
    for block in range(4):
        w = (p_ref[8 * block : 8 * block + 8].reshape(1024, 1024) * by).astype(jnp.bfloat16)
        total = total + score(own_values(kvs, head, block), w)
    whole, _ = joined(near_ref[head], far_ref[head])
    result = (total + whole[0:64] / whole[64:65]).astype(jnp.bfloat16)
    for z in range(8):
        out_ref[z, head] = result[:, 128 * z : 128 * z + 128]


def own_weights(head, q_ref, kvs, p_ref):
    upper, lower = both_places(jnp.concatenate([q_ref[z, head] for z in range(8)], axis=1))
    sums = jnp.zeros((8, 1024), jnp.float32)
    for block in range(4):
        for side, place in enumerate((upper, lower)):
            p = jnp.exp2(score(own_keys(kvs, head, block), place) * EXP2_SCALE)
            p_ref[8 * block : 8 * block + 8, 64 * side : 64 * side + 64] = p.reshape(8, 64, 1024)
            sums = sums + jnp.sum(p.reshape(-1, 8, 1024), axis=0)
    return jnp.sum(sums, axis=0, keepdims=True)


def own_shifted(head, q_ref, kvs, p_ref, sum_ref):
    def one(i, carry):
        span = pl.ds(pl.multiple_of(i * 256, 256), 256)
        places = both_places(jnp.concatenate([q_ref[2 * i, head], q_ref[2 * i + 1, head]], axis=1))
        top = jnp.full((8, 256), -jnp.inf, jnp.float32)
        for block, kv in enumerate(kvs):

            def scored(c, top):
                for side, place in enumerate(places):
                    a = score(kv[c, head, 0:64], place)
                    p_ref[8 * block + c, 64 * side : 64 * side + 64, span] = a
                    top = jnp.maximum(top, peak(a))
                return top

            top = lax.fori_loop(0, 8, scored, top)
        top = jnp.max(top, axis=0, keepdims=True)

        def weighed(c, sums):
            p = jnp.exp2((p_ref[c, :, span] - top) * EXP2_SCALE)
            p_ref[c, :, span] = p
            return sums + jnp.sum(p.reshape(16, 8, 256), axis=0)

        sums = lax.fori_loop(0, 32, weighed, jnp.zeros((8, 256), jnp.float32))
        sum_ref[head, 0:1, span] = jnp.sum(sums, axis=0, keepdims=True)
        return carry

    lax.fori_loop(0, 4, one, 0)


def own_kernel(q_ref, kv0, kv1, kv2, kv3, near_ref, far_ref, out_ref, p_ref, sum_ref):
    kvs = (kv0, kv1, kv2, kv3)
    rest = kvs, near_ref, far_ref, out_ref, p_ref

    def whole(head):
        sum_ref[head, 0:1] = own_weights(head, q_ref, kvs, p_ref)

        @pl.when(outside(sum_ref[head, 0:1]))
        def _():
            own_shifted(head, q_ref, kvs, p_ref, sum_ref)

        own_finish(head, *rest, sum_ref[head, 0:1])

    each_head(3, whole)


def cross_attend(q, rows, before=None, wait=None, token=False):
    others = [array for array in (before, wait) if array is not None]
    return pl.pallas_call(
        functools.partial(cross_kernel, len(rows), before is not None, token),
        out_shape=[jax.ShapeDtypeStruct((8, 128), jnp.float32)] * token
        + [jax.ShapeDtypeStruct((3, 80, 1024), jnp.float32)],
        compiler_params=PARAMS,
        name="cross",
    )(q, *rows, *others)


def split_kernel(own_ref, q_ref, kv_ref):
    q_ref[...] = own_ref[:, :, 0:64]
    kv_ref[...] = own_ref[:, :, 64:192]


def split(own):
    return pl.pallas_call(
        split_kernel,
        out_shape=(
            jax.ShapeDtypeStruct((8, 3, 64, 128), jnp.bfloat16),
            jax.ShapeDtypeStruct((8, 3, 128, 128), jnp.bfloat16),
        ),
        compiler_params=PARAMS,
        name="split",
    )(own)


def own_attend(q, column, near, far):
    return pl.pallas_call(
        own_kernel,
        out_shape=jax.ShapeDtypeStruct((8, 3, 64, 128), jnp.bfloat16),
        scratch_shapes=[
            pltpu.VMEM((32, 128, 1024), jnp.float32),
            pltpu.VMEM((3, 8, 1024), jnp.float32),
        ],
        compiler_params=OWN_PARAMS,
        name="own",
    )(q, *column, near, far)


def project_kernel(heads_ref, w_ref, hidden_ref, gate_ref, out_ref):
    rows = jnp.concatenate(
        [heads_ref[128 * j : 128 * j + 128].T for j in range(12)], axis=1
    )
    projected = jnp.dot(rows, w_ref[...], preferred_element_type=jnp.float32)
    out_ref[...] = (hidden_ref[...].astype(jnp.float32) + gate_ref[...] * projected).astype(
        jnp.bfloat16
    )


def project(heads, w_out, hidden, gate):
    return pl.pallas_call(
        project_kernel,
        out_shape=jax.ShapeDtypeStruct((128, 1536), jnp.bfloat16),
        compiler_params=PARAMS,
        name="project",
    )(heads, w_out, hidden, gate)


def shifted(array, axis, size, step):
    return lax.ppermute(array, axis, [(i, (i + step) % size) for i in range(size)])


def body(queries, keys, values, hidden_in, gate, w_out):
    x, y = ("xh", "xl"), "y"
    pool, own = prep(queries[0], keys[0], values[0])
    pool = lax.all_to_all(pool, "z", 0, 0, tiled=True)
    own = lax.all_to_all(own, "z", 0, 0, tiled=True)
    piece = repack(pool)
    row = jnp.stack([piece] + [shifted(piece, x, 4, step) for step in (1, 3, 2)], axis=1)
    back, ahead = shifted(row, y, 4, 1), shifted(row, y, 4, 3)
    across = shifted(back, y, 4, 1)
    q, kv = split(own)
    kv_x = shifted(kv, "xl", 2, 1)
    column = [kv, shifted(kv, "core", 2, 1), kv_x, shifted(kv_x, "core", 2, 1)]
    q_far = shifted(q, "core", 2, 1)
    token, near = cross_attend(q, [row, back, ahead], token=True)
    (far,) = cross_attend(q_far, [row, back, ahead], wait=token)
    token, far = cross_attend(q_far, [across], before=far, token=True)
    far = shifted(far, "core", 2, 1)
    (near,) = cross_attend(q, [across], before=near, wait=token)
    heads = own_attend(q, column, near, far)
    returned = lax.all_to_all(heads, "z", 0, 0, tiled=True)
    result = project(returned.reshape(1536, 128), w_out, hidden_in[0], gate)
    return result[None]


def solution(mesh):
    fine = Mesh(mesh.devices.reshape(SIZES), AXES)
    tokens = P(("y", "xh"), ("xl", "z", "core"), None)
    placed = (tokens, tokens, tokens, tokens, P(("y", "xh"), None), P())
    return jax.shard_map(body, mesh=fine, in_specs=placed, out_specs=tokens, check_vma=False)
```

```python
import functools
import math

import jax
import jax.numpy as jnp
from jax import lax
from jax.experimental import pallas as pl
from jax.experimental.pallas import tpu as pltpu
from jax.sharding import Mesh, PartitionSpec as P

EXP2_SCALE = math.log2(math.e) / 8.0
VMEM = 20 * 2**20
OWN_PARAMS = pltpu.CompilerParams(vmem_limit_bytes=32 * 2**20)
PREP_PARAMS = pltpu.CompilerParams(vmem_limit_bytes=60 * 2**20)
PARAMS = pltpu.CompilerParams(vmem_limit_bytes=VMEM)
LEAST, MOST = 2.0**-64, 2.0**64
AXES = ("y", "xh", "xl", "z", "core")
SIZES = (4, 2, 2, 8, 2)


def swap_halves(tile):
    return jnp.concatenate([tile[:, 64:], tile[:, :64]], axis=1)


def pair_heads(tile):
    half = tile.shape[0] // 2
    upper, lower = tile[:half], tile[half:]
    first = jnp.concatenate([upper[:, :64], lower[:, :64]], axis=1)
    second = jnp.concatenate([upper[:, 64:], lower[:, 64:]], axis=1)
    return first, second


def prep_kernel(q_ref, k_ref, v_ref, pool_ref, own_ref):
    rows = lax.broadcasted_iota(jnp.int32, (32, 128), 0)
    cols = lax.broadcasted_iota(jnp.int32, (32, 128), 1)
    mean4 = jnp.where(cols // 4 == rows, 0.25, 0.0).astype(jnp.bfloat16)
    for j in range(12):
        span = pl.ds(j * 128, 128)
        q, k, v = q_ref[:, span], k_ref[:, span], v_ref[:, span]
        qt, vt = q.T, v.T
        packed_k = pair_heads(k)
        pooled_k = pair_heads(
            jnp.dot(mean4, k, preferred_element_type=jnp.float32).astype(jnp.bfloat16)
        )
        pooled_v = pair_heads(
            jnp.dot(mean4, v, preferred_element_type=jnp.float32).astype(jnp.bfloat16)
        )
        for side in range(2):
            group, member = divmod(2 * j + side, 3)
            own_ref[group, member, 0:64] = qt[side * 64 : side * 64 + 64]
            own_ref[group, member, 64:128] = packed_k[side]
            own_ref[group, member, 128:192] = vt[side * 64 : side * 64 + 64]
            pool_ref[group, 0, member] = pooled_k[side]
            pool_ref[group, 1, member] = pooled_v[side]


def prep(q, k, v):
    return pl.pallas_call(
        prep_kernel,
        out_shape=(
            jax.ShapeDtypeStruct((8, 2, 3, 16, 128), jnp.bfloat16),
            jax.ShapeDtypeStruct((8, 3, 192, 128), jnp.bfloat16),
        ),
        compiler_params=PREP_PARAMS,
        name="prep",
    )(q, k, v)


def repack_kernel(pool_ref, out_ref):
    for member in range(3):
        out_ref[0, member] = pool_ref[:, 0, member].reshape(128, 128)
        out_ref[1, member] = pool_ref[:, 1, member].reshape(128, 128).T


def repack(pool):
    return pl.pallas_call(
        repack_kernel,
        out_shape=jax.ShapeDtypeStruct((2, 3, 128, 128), jnp.bfloat16),
        compiler_params=PARAMS,
        name="repack",
    )(pool)


def both_places(qt):
    zero = jnp.zeros_like(qt)
    return jnp.concatenate([qt, zero], axis=0), jnp.concatenate([zero, qt], axis=0)


def score(keys, queries):
    return jnp.dot(keys, queries, preferred_element_type=jnp.float32)


def outside(totals):
    return jnp.logical_not((jnp.min(totals) > LEAST) & (jnp.max(totals) < MOST))


def peak(a):
    return jnp.max(a.reshape(-1, 8, a.shape[1]), axis=0)


def joined(near, far):
    most = jnp.maximum(near[72:73], far[72:73])
    near_by = jnp.exp2((near[72:73] - most) * EXP2_SCALE)
    far_by = jnp.exp2((far[72:73] - most) * EXP2_SCALE)
    return near[0:72] * near_by + far[0:72] * far_by, most


def row_keys(row, head):
    return row[0, :, head].reshape(512, 128)


def row_weighted(row, head, p):
    parts = [row[1, x, head] for x in range(4)]
    values = jnp.concatenate([v[:64] for v in parts] + [v[64:] for v in parts], axis=1)
    ones = jnp.ones((16, 1024), jnp.bfloat16)
    return score(jnp.concatenate([values, ones], axis=0), p)


def cross_head(head, q_ref, rows, out_ref):
    upper, lower = both_places(jnp.concatenate([q_ref[z, head] for z in range(8)], axis=1))
    total = jnp.zeros((80, 1024), jnp.float32)
    for row in rows:
        p = [
            jnp.exp2(score(row_keys(row, head), place) * EXP2_SCALE).astype(jnp.bfloat16)
            for place in (upper, lower)
        ]
        total = total + row_weighted(row, head, jnp.concatenate(p, axis=0))
    out_ref[head, 0:72] = total[0:72]
    out_ref[head, 72:80] = jnp.zeros((8, 1024), jnp.float32)


def cross_shifted(head, q_ref, rows, out_ref):
    def one(i, carry):
        places = both_places(jnp.concatenate([q_ref[2 * i, head], q_ref[2 * i + 1, head]], axis=1))
        span = pl.ds(pl.multiple_of(i * 256, 256), 256)
        ones = jnp.ones((16, 256), jnp.bfloat16)
        out_ref[head, 0:72, span] = jnp.zeros((72, 256), jnp.float32)
        out_ref[head, 72:80, span] = jnp.full((8, 256), -jnp.inf, jnp.float32)
        for row in rows:

            def some(x, carry):
                a = jnp.concatenate([score(row[0, x, head], place) for place in places], axis=0)
                top = out_ref[head, 72:73, span]
                newer = jnp.maximum(top, jnp.max(peak(a), axis=0, keepdims=True))
                p = jnp.exp2((a - newer) * EXP2_SCALE).astype(jnp.bfloat16)
                v = row[1, x, head]
                values = jnp.concatenate([jnp.concatenate([v[:64], v[64:]], axis=1), ones], axis=0)
                total = out_ref[head, 0:72, span] * jnp.exp2((top - newer) * EXP2_SCALE)
                out_ref[head, 0:72, span] = total + score(values, p)[0:72]
                out_ref[head, 72:80, span] = jnp.broadcast_to(newer, (8, 256))
                return carry

            lax.fori_loop(0, 4, some, 0)
        return carry

    lax.fori_loop(0, 4, one, 0)


def each_head(count, step, unroll=False):
    if unroll:
        for head in range(count):
            step(head)
    else:
        lax.fori_loop(0, count, lambda head, carry: (step(head), carry)[1], 0)


def cross_kernel(count, has_before, has_token, handed, q_ref, *refs):
    rows, out_ref = refs[:count], refs[-1]
    if handed:
        refs[-2][...] = rows[-1][...]
    if has_token:
        refs[-2][...] = jnp.zeros((8, 128), jnp.float32)
    each_head(3, lambda head: cross_head(head, q_ref, rows, out_ref))

    @pl.when(outside(out_ref[:, 64:65]))
    def _():
        each_head(3, lambda head: cross_shifted(head, q_ref, rows, out_ref))

    def join(head):
        whole, most = joined(out_ref[head], refs[count][head])
        out_ref[head, 0:72] = whole
        out_ref[head, 72:80] = jnp.broadcast_to(most, (8, 1024))

    if has_before:
        each_head(3, join)


def own_keys(kvs, head, block):
    return kvs[block][:, head, 0:64].reshape(512, 128)


def own_values(kvs, head, block):
    return jnp.concatenate([kvs[block][c, head, 64:128] for c in range(8)], axis=1)


def own_finish(head, kvs, near_ref, far_ref, out_ref, p_ref, sums):
    by = 1.0 / sums
    total = jnp.zeros((64, 1024), jnp.float32)
    for block in range(4):
        w = (p_ref[8 * block : 8 * block + 8].reshape(1024, 1024) * by).astype(jnp.bfloat16)
        total = total + score(own_values(kvs, head, block), w)
    whole, _ = joined(near_ref[head], far_ref[head])
    result = (total + whole[0:64] / whole[64:65]).astype(jnp.bfloat16)
    for z in range(8):
        out_ref[z, head] = result[:, 128 * z : 128 * z + 128]


def own_weights(head, q_ref, kvs, p_ref):
    upper, lower = both_places(jnp.concatenate([q_ref[z, head] for z in range(8)], axis=1))
    sums = jnp.zeros((8, 1024), jnp.float32)
    for block in range(4):
        for side, place in enumerate((upper, lower)):
            p = jnp.exp2(score(own_keys(kvs, head, block), place) * EXP2_SCALE)
            p_ref[8 * block : 8 * block + 8, 64 * side : 64 * side + 64] = p.reshape(8, 64, 1024)
            sums = sums + jnp.sum(p.reshape(-1, 8, 1024), axis=0)
    return jnp.sum(sums, axis=0, keepdims=True)


def own_shifted(head, q_ref, kvs, p_ref, sum_ref):
    def one(i, carry):
        span = pl.ds(pl.multiple_of(i * 256, 256), 256)
        places = both_places(jnp.concatenate([q_ref[2 * i, head], q_ref[2 * i + 1, head]], axis=1))
        top = jnp.full((8, 256), -jnp.inf, jnp.float32)
        for block, kv in enumerate(kvs):

            def scored(c, top):
                for side, place in enumerate(places):
                    a = score(kv[c, head, 0:64], place)
                    p_ref[8 * block + c, 64 * side : 64 * side + 64, span] = a
                    top = jnp.maximum(top, peak(a))
                return top

            top = lax.fori_loop(0, 8, scored, top)
        top = jnp.max(top, axis=0, keepdims=True)

        def weighed(c, sums):
            p = jnp.exp2((p_ref[c, :, span] - top) * EXP2_SCALE)
            p_ref[c, :, span] = p
            return sums + jnp.sum(p.reshape(16, 8, 256), axis=0)

        sums = lax.fori_loop(0, 32, weighed, jnp.zeros((8, 256), jnp.float32))
        sum_ref[head, 0:1, span] = jnp.sum(sums, axis=0, keepdims=True)
        return carry

    lax.fori_loop(0, 4, one, 0)


def own_kernel(q_ref, kv0, kv1, kv2, kv3, near_ref, far_ref, out_ref, p_ref, sum_ref):
    kvs = (kv0, kv1, kv2, kv3)
    rest = kvs, near_ref, far_ref, out_ref, p_ref

    def whole(head):
        sum_ref[head, 0:1] = own_weights(head, q_ref, kvs, p_ref)

        @pl.when(outside(sum_ref[head, 0:1]))
        def _():
            own_shifted(head, q_ref, kvs, p_ref, sum_ref)

        own_finish(head, *rest, sum_ref[head, 0:1])

    each_head(3, whole)


def cross_attend(q, rows, before=None, wait=None, token=False, hand_on=False):
    others = [array for array in (before, wait) if array is not None]
    return pl.pallas_call(
        functools.partial(cross_kernel, len(rows), before is not None, token, hand_on),
        out_shape=[jax.ShapeDtypeStruct((8, 128), jnp.float32)] * token
        + [jax.ShapeDtypeStruct(rows[-1].shape, jnp.bfloat16)] * hand_on
        + [jax.ShapeDtypeStruct((3, 80, 1024), jnp.float32)],
        compiler_params=PARAMS,
        name="cross",
    )(q, *rows, *others)


def split_kernel(own_ref, q_ref, kv_ref):
    q_ref[...] = own_ref[:, :, 0:64]
    kv_ref[...] = own_ref[:, :, 64:192]


def split(own):
    return pl.pallas_call(
        split_kernel,
        out_shape=(
            jax.ShapeDtypeStruct((8, 3, 64, 128), jnp.bfloat16),
            jax.ShapeDtypeStruct((8, 3, 128, 128), jnp.bfloat16),
        ),
        compiler_params=PARAMS,
        name="split",
    )(own)


def own_attend(q, column, near, far):
    return pl.pallas_call(
        own_kernel,
        out_shape=jax.ShapeDtypeStruct((8, 3, 64, 128), jnp.bfloat16),
        scratch_shapes=[
            pltpu.VMEM((32, 128, 1024), jnp.float32),
            pltpu.VMEM((3, 8, 1024), jnp.float32),
        ],
        compiler_params=OWN_PARAMS,
        name="own",
    )(q, *column, near, far)


def project_kernel(heads_ref, w_ref, hidden_ref, gate_ref, out_ref):
    rows = jnp.concatenate(
        [heads_ref[128 * j : 128 * j + 128].T for j in range(12)], axis=1
    )
    projected = jnp.dot(rows, w_ref[...], preferred_element_type=jnp.float32)
    out_ref[...] = (hidden_ref[...].astype(jnp.float32) + gate_ref[...] * projected).astype(
        jnp.bfloat16
    )


def project(heads, w_out, hidden, gate):
    return pl.pallas_call(
        project_kernel,
        out_shape=jax.ShapeDtypeStruct((128, 1536), jnp.bfloat16),
        compiler_params=PARAMS,
        name="project",
    )(heads, w_out, hidden, gate)


def shifted(array, axis, size, step):
    return lax.ppermute(array, axis, [(i, (i + step) % size) for i in range(size)])


def body(queries, keys, values, hidden_in, gate, w_out):
    x, y = ("xh", "xl"), "y"
    pool, own = prep(queries[0], keys[0], values[0])
    pool = lax.all_to_all(pool, "z", 0, 0, tiled=True)
    own = lax.all_to_all(own, "z", 0, 0, tiled=True)
    piece = repack(pool)
    row = jnp.stack([piece] + [shifted(piece, x, 4, step) for step in (1, 3, 2)], axis=1)
    back, ahead = shifted(row, y, 4, 1), shifted(row, y, 4, 3)
    across = shifted(back, y, 4, 1)
    q, kv = split(own)
    kv_x = shifted(kv, "xl", 2, 1)
    column = [kv, shifted(kv, "core", 2, 1), kv_x, shifted(kv_x, "core", 2, 1)]
    q_far = shifted(q, "core", 2, 1)
    ahead, near = cross_attend(q, [row, back, ahead], hand_on=True)
    (far,) = cross_attend(q_far, [row, back, ahead])
    token, far = cross_attend(q_far, [across], before=far, token=True)
    far = shifted(far, "core", 2, 1)
    (near,) = cross_attend(q, [across], before=near, wait=token)
    heads = own_attend(q, column, near, far)
    returned = lax.all_to_all(heads, "z", 0, 0, tiled=True)
    result = project(returned.reshape(1536, 128), w_out, hidden_in[0], gate)
    return result[None]


def solution(mesh):
    fine = Mesh(mesh.devices.reshape(SIZES), AXES)
    tokens = P(("y", "xh"), ("xl", "z", "core"), None)
    placed = (tokens, tokens, tokens, tokens, P(("y", "xh"), None), P())
    return jax.shard_map(body, mesh=fine, in_specs=placed, out_specs=tokens, check_vma=False)
```

```python
import functools
import math

import jax
import jax.numpy as jnp
from jax import lax
from jax.experimental import pallas as pl
from jax.experimental.pallas import tpu as pltpu
from jax.sharding import Mesh, PartitionSpec as P

EXP2_SCALE = math.log2(math.e) / 8.0
VMEM = 20 * 2**20
OWN_PARAMS = pltpu.CompilerParams(vmem_limit_bytes=32 * 2**20)
PREP_PARAMS = pltpu.CompilerParams(vmem_limit_bytes=60 * 2**20)
PARAMS = pltpu.CompilerParams(vmem_limit_bytes=VMEM)
LEAST, MOST = 2.0**-64, 2.0**64
AXES = ("y", "xh", "xl", "z", "core")
SIZES = (4, 2, 2, 8, 2)


def swap_halves(tile):
    return jnp.concatenate([tile[:, 64:], tile[:, :64]], axis=1)


def pair_heads(tile):
    half = tile.shape[0] // 2
    upper, lower = tile[:half], tile[half:]
    first = jnp.concatenate([upper[:, :64], lower[:, :64]], axis=1)
    second = jnp.concatenate([upper[:, 64:], lower[:, 64:]], axis=1)
    return first, second


def prep_kernel(q_ref, k_ref, v_ref, pool_ref, own_ref):
    rows = lax.broadcasted_iota(jnp.int32, (32, 128), 0)
    cols = lax.broadcasted_iota(jnp.int32, (32, 128), 1)
    mean4 = jnp.where(cols // 4 == rows, 0.25, 0.0).astype(jnp.bfloat16)
    for j in range(12):
        span = pl.ds(j * 128, 128)
        q, k, v = q_ref[:, span], k_ref[:, span], v_ref[:, span]
        qt, vt = q.T, v.T
        packed_k = pair_heads(k)
        pooled_k = pair_heads(
            jnp.dot(mean4, k, preferred_element_type=jnp.float32).astype(jnp.bfloat16)
        )
        pooled_v = pair_heads(
            jnp.dot(mean4, v, preferred_element_type=jnp.float32).astype(jnp.bfloat16)
        )
        for side in range(2):
            group, member = divmod(2 * j + side, 3)
            own_ref[group, member, 0:64] = qt[side * 64 : side * 64 + 64]
            own_ref[group, member, 64:128] = packed_k[side]
            own_ref[group, member, 128:192] = vt[side * 64 : side * 64 + 64]
            pool_ref[group, 0, member] = pooled_k[side]
            pool_ref[group, 1, member] = pooled_v[side]


def prep(q, k, v):
    return pl.pallas_call(
        prep_kernel,
        out_shape=(
            jax.ShapeDtypeStruct((8, 2, 3, 16, 128), jnp.bfloat16),
            jax.ShapeDtypeStruct((8, 3, 192, 128), jnp.bfloat16),
        ),
        compiler_params=PREP_PARAMS,
        name="prep",
    )(q, k, v)


def repack_kernel(pool_ref, out_ref):
    for member in range(3):
        out_ref[0, member] = pool_ref[:, 0, member].reshape(128, 128)
        out_ref[1, member] = pool_ref[:, 1, member].reshape(128, 128).T


def repack(pool):
    return pl.pallas_call(
        repack_kernel,
        out_shape=jax.ShapeDtypeStruct((2, 3, 128, 128), jnp.bfloat16),
        compiler_params=PARAMS,
        name="repack",
    )(pool)


def both_places(qt):
    zero = jnp.zeros_like(qt)
    return jnp.concatenate([qt, zero], axis=0), jnp.concatenate([zero, qt], axis=0)


def score(keys, queries):
    return jnp.dot(keys, queries, preferred_element_type=jnp.float32)


def outside(totals):
    return jnp.logical_not((jnp.min(totals) > LEAST) & (jnp.max(totals) < MOST))


def peak(a):
    return jnp.max(a.reshape(-1, 8, a.shape[1]), axis=0)


def joined(near, far):
    most = jnp.maximum(near[72:73], far[72:73])
    near_by = jnp.exp2((near[72:73] - most) * EXP2_SCALE)
    far_by = jnp.exp2((far[72:73] - most) * EXP2_SCALE)
    return near[0:72] * near_by + far[0:72] * far_by, most


def row_keys(row, head):
    return row[0, :, head].reshape(512, 128)


def row_weighted(row, head, p):
    parts = [row[1, x, head] for x in range(4)]
    values = jnp.concatenate([v[:64] for v in parts] + [v[64:] for v in parts], axis=1)
    ones = jnp.ones((16, 1024), jnp.bfloat16)
    return score(jnp.concatenate([values, ones], axis=0), p)


def cross_head(head, q_ref, rows, out_ref):
    upper, lower = both_places(jnp.concatenate([q_ref[z, head] for z in range(8)], axis=1))
    total = jnp.zeros((80, 1024), jnp.float32)
    for row in rows:
        p = [
            jnp.exp2(score(row_keys(row, head), place) * EXP2_SCALE).astype(jnp.bfloat16)
            for place in (upper, lower)
        ]
        total = total + row_weighted(row, head, jnp.concatenate(p, axis=0))
    out_ref[head, 0:72] = total[0:72]
    out_ref[head, 72:80] = jnp.zeros((8, 1024), jnp.float32)


def cross_shifted(head, q_ref, rows, out_ref):
    def one(i, carry):
        places = both_places(jnp.concatenate([q_ref[2 * i, head], q_ref[2 * i + 1, head]], axis=1))
        span = pl.ds(pl.multiple_of(i * 256, 256), 256)
        ones = jnp.ones((16, 256), jnp.bfloat16)
        out_ref[head, 0:72, span] = jnp.zeros((72, 256), jnp.float32)
        out_ref[head, 72:80, span] = jnp.full((8, 256), -jnp.inf, jnp.float32)
        for row in rows:

            def some(x, carry):
                a = jnp.concatenate([score(row[0, x, head], place) for place in places], axis=0)
                top = out_ref[head, 72:73, span]
                newer = jnp.maximum(top, jnp.max(peak(a), axis=0, keepdims=True))
                p = jnp.exp2((a - newer) * EXP2_SCALE).astype(jnp.bfloat16)
                v = row[1, x, head]
                values = jnp.concatenate([jnp.concatenate([v[:64], v[64:]], axis=1), ones], axis=0)
                total = out_ref[head, 0:72, span] * jnp.exp2((top - newer) * EXP2_SCALE)
                out_ref[head, 0:72, span] = total + score(values, p)[0:72]
                out_ref[head, 72:80, span] = jnp.broadcast_to(newer, (8, 256))
                return carry

            lax.fori_loop(0, 4, some, 0)
        return carry

    lax.fori_loop(0, 4, one, 0)


def each_head(count, step, unroll=False):
    if unroll:
        for head in range(count):
            step(head)
    else:
        lax.fori_loop(0, count, lambda head, carry: (step(head), carry)[1], 0)


def cross_kernel(count, has_before, has_token, handed, q_ref, *refs):
    rows, out_ref = refs[:count], refs[-1]
    if handed:
        refs[-2][...] = rows[-1][...]
    if has_token:
        refs[-2][...] = jnp.zeros((8, 128), jnp.float32)
    each_head(3, lambda head: cross_head(head, q_ref, rows, out_ref))

    @pl.when(outside(out_ref[:, 64:65]))
    def _():
        each_head(3, lambda head: cross_shifted(head, q_ref, rows, out_ref))

    def join(head):
        whole, most = joined(out_ref[head], refs[count][head])
        out_ref[head, 0:72] = whole
        out_ref[head, 72:80] = jnp.broadcast_to(most, (8, 1024))

    if has_before:
        each_head(3, join)


def own_keys(kvs, head, block):
    return kvs[block][:, head, 0:64].reshape(512, 128)


def own_values(kvs, head, block):
    return jnp.concatenate([kvs[block][c, head, 64:128] for c in range(8)], axis=1)


def own_finish(head, kvs, near_ref, far_ref, out_ref, p_ref, sums):
    by = 1.0 / sums
    total = jnp.zeros((64, 1024), jnp.float32)
    for block in range(4):
        w = (p_ref[8 * block : 8 * block + 8].reshape(1024, 1024) * by).astype(jnp.bfloat16)
        total = total + score(own_values(kvs, head, block), w)
    whole, _ = joined(near_ref[head], far_ref[head])
    result = (total + whole[0:64] / whole[64:65]).astype(jnp.bfloat16)
    for z in range(8):
        out_ref[z, head] = result[:, 128 * z : 128 * z + 128]


def own_weights(head, q_ref, kvs, p_ref):
    upper, lower = both_places(jnp.concatenate([q_ref[z, head] for z in range(8)], axis=1))
    sums = jnp.zeros((8, 1024), jnp.float32)
    for block in range(4):
        for side, place in enumerate((upper, lower)):
            p = jnp.exp2(score(own_keys(kvs, head, block), place) * EXP2_SCALE)
            p_ref[8 * block : 8 * block + 8, 64 * side : 64 * side + 64] = p.reshape(8, 64, 1024)
            sums = sums + jnp.sum(p.reshape(-1, 8, 1024), axis=0)
    return jnp.sum(sums, axis=0, keepdims=True)


def own_shifted(head, q_ref, kvs, p_ref, sum_ref):
    def one(i, carry):
        span = pl.ds(pl.multiple_of(i * 256, 256), 256)
        places = both_places(jnp.concatenate([q_ref[2 * i, head], q_ref[2 * i + 1, head]], axis=1))
        top = jnp.full((8, 256), -jnp.inf, jnp.float32)
        for block, kv in enumerate(kvs):

            def scored(c, top):
                for side, place in enumerate(places):
                    a = score(kv[c, head, 0:64], place)
                    p_ref[8 * block + c, 64 * side : 64 * side + 64, span] = a
                    top = jnp.maximum(top, peak(a))
                return top

            top = lax.fori_loop(0, 8, scored, top)
        top = jnp.max(top, axis=0, keepdims=True)

        def weighed(c, sums):
            p = jnp.exp2((p_ref[c, :, span] - top) * EXP2_SCALE)
            p_ref[c, :, span] = p
            return sums + jnp.sum(p.reshape(16, 8, 256), axis=0)

        sums = lax.fori_loop(0, 32, weighed, jnp.zeros((8, 256), jnp.float32))
        sum_ref[head, 0:1, span] = jnp.sum(sums, axis=0, keepdims=True)
        return carry

    lax.fori_loop(0, 4, one, 0)


def own_kernel(q_ref, kv0, kv1, kv2, kv3, near_ref, far_ref, out_ref, p_ref, sum_ref):
    kvs = (kv0, kv1, kv2, kv3)
    rest = kvs, near_ref, far_ref, out_ref, p_ref

    def plain(head):
        sums = own_weights(head, q_ref, kvs, p_ref)
        sum_ref[head, 0:1] = sums
        own_finish(head, *rest, sums)

    each_head(3, plain)

    @pl.when(outside(sum_ref[:, 0:1]))
    def _():
        def again(head):
            own_shifted(head, q_ref, kvs, p_ref, sum_ref)
            own_finish(head, *rest, sum_ref[head, 0:1])

        each_head(3, again)


def cross_attend(q, rows, before=None, wait=None, token=False, hand_on=False):
    others = [array for array in (before, wait) if array is not None]
    return pl.pallas_call(
        functools.partial(cross_kernel, len(rows), before is not None, token, hand_on),
        out_shape=[jax.ShapeDtypeStruct((8, 128), jnp.float32)] * token
        + [jax.ShapeDtypeStruct(rows[-1].shape, jnp.bfloat16)] * hand_on
        + [jax.ShapeDtypeStruct((3, 80, 1024), jnp.float32)],
        compiler_params=PARAMS,
        name="cross",
    )(q, *rows, *others)


def split_kernel(own_ref, q_ref, kv_ref):
    q_ref[...] = own_ref[:, :, 0:64]
    kv_ref[...] = own_ref[:, :, 64:192]


def split(own):
    return pl.pallas_call(
        split_kernel,
        out_shape=(
            jax.ShapeDtypeStruct((8, 3, 64, 128), jnp.bfloat16),
            jax.ShapeDtypeStruct((8, 3, 128, 128), jnp.bfloat16),
        ),
        compiler_params=PARAMS,
        name="split",
    )(own)


def own_attend(q, column, near, far):
    return pl.pallas_call(
        own_kernel,
        out_shape=jax.ShapeDtypeStruct((8, 3, 64, 128), jnp.bfloat16),
        scratch_shapes=[
            pltpu.VMEM((32, 128, 1024), jnp.float32),
            pltpu.VMEM((3, 8, 1024), jnp.float32),
        ],
        compiler_params=OWN_PARAMS,
        name="own",
    )(q, *column, near, far)


def project_kernel(heads_ref, w_ref, hidden_ref, gate_ref, out_ref):
    rows = jnp.concatenate(
        [heads_ref[128 * j : 128 * j + 128].T for j in range(12)], axis=1
    )
    projected = jnp.dot(rows, w_ref[...], preferred_element_type=jnp.float32)
    out_ref[...] = (hidden_ref[...].astype(jnp.float32) + gate_ref[...] * projected).astype(
        jnp.bfloat16
    )


def project(heads, w_out, hidden, gate):
    return pl.pallas_call(
        project_kernel,
        out_shape=jax.ShapeDtypeStruct((128, 1536), jnp.bfloat16),
        compiler_params=PARAMS,
        name="project",
    )(heads, w_out, hidden, gate)


def shifted(array, axis, size, step):
    return lax.ppermute(array, axis, [(i, (i + step) % size) for i in range(size)])


def body(queries, keys, values, hidden_in, gate, w_out):
    x, y = ("xh", "xl"), "y"
    pool, own = prep(queries[0], keys[0], values[0])
    pool = lax.all_to_all(pool, "z", 0, 0, tiled=True)
    own = lax.all_to_all(own, "z", 0, 0, tiled=True)
    piece = repack(pool)
    row = jnp.stack([piece] + [shifted(piece, x, 4, step) for step in (1, 3, 2)], axis=1)
    back, ahead = shifted(row, y, 4, 1), shifted(row, y, 4, 3)
    across = shifted(back, y, 4, 1)
    q, kv = split(own)
    kv_x = shifted(kv, "xl", 2, 1)
    column = [kv, shifted(kv, "core", 2, 1), kv_x, shifted(kv_x, "core", 2, 1)]
    q_far = shifted(q, "core", 2, 1)
    ahead, near = cross_attend(q, [row, back, ahead], hand_on=True)
    (far,) = cross_attend(q_far, [row, back, ahead])
    token, far = cross_attend(q_far, [across], before=far, token=True)
    far = shifted(far, "core", 2, 1)
    (near,) = cross_attend(q, [across], before=near, wait=token)
    heads = own_attend(q, column, near, far)
    returned = lax.all_to_all(heads, "z", 0, 0, tiled=True)
    result = project(returned.reshape(1536, 128), w_out, hidden_in[0], gate)
    return result[None]


def solution(mesh):
    fine = Mesh(mesh.devices.reshape(SIZES), AXES)
    tokens = P(("y", "xh"), ("xl", "z", "core"), None)
    placed = (tokens, tokens, tokens, tokens, P(("y", "xh"), None), P())
    return jax.shard_map(body, mesh=fine, in_specs=placed, out_specs=tokens, check_vma=False)
```
